32 devices in a mesh: row: 8 (over y, x, core), col: 4 (over z).
Axes of the slice: x: 2, y: 2, z: 4, core: 2. Of those that a mesh axis runs over, the one named last changes fastest.
Arguments:
- first_view: bfloat16 [512, 16384], P(None, 'row'), may hold values from -20 to 20
- second_view: bfloat16 [512, 16384], P(None, 'row'), may hold values from -20 to 20
- projector: bfloat16 [16384, 16384], P('row', 'col'), may hold values from -1 to 1
Outputs:
- grad_first: float32 [512, 4, 8, 512], P(None, 'col', 'row')
- grad_second: float32 [512, 4, 8, 512], P(None, 'col', 'row')
- correlation: float32 [4, 8, 512, 16384], P(None, 'row', None, 'col')
The draws below stay inside these ranges and needn't reach their ends.
All inputs are finite; a program needn't handle non-finite values.
Results may differ from the reference program's by a relative error of at most 0.0003.
Values sent between devices are 32-bit elements; how exact they have to be, the bound alone decides.
A program may use at most 128 MiB of HBM per device.

```python
import math
import jax
import jax.numpy as jnp
from jax import lax

BATCH = 512
PROJ = 16384
N_ROW = 8
N_COL = 4


def draw_first_view(key, part):
    key = jax.random.fold_in(key, 11)
    key_base, key_mean = jax.random.split(key, 2)
    means = jax.random.uniform(key_mean, (1, PROJ), jnp.float32, -1.0, 1.0)
    base = jax.random.truncated_normal(key_base, -4.0, 4.0, (BATCH, PROJ), jnp.float32)
    return (base + means).astype(jnp.bfloat16)


def draw_second_view(key, part):
    key = jax.random.fold_in(key, 12)
    key_base, key_mean = jax.random.split(key, 2)
    means = jax.random.uniform(key_mean, (1, PROJ), jnp.float32, -1.0, 1.0)
    base = jax.random.truncated_normal(key_base, -4.0, 4.0, (BATCH, PROJ), jnp.float32)
    return (base + means).astype(jnp.bfloat16)


def draw_projector(key, part):
    key = jax.random.fold_in(key, 13)
    key_base, key_scale = jax.random.split(key, 2)
    base = jax.random.truncated_normal(key_base, -4.0, 4.0, (PROJ, PROJ), jnp.float32)
    scales = jnp.exp(jax.random.uniform(key_scale, (1, PROJ), jnp.float32, 0.0, math.log(10.0)))
    return (base * scales / math.sqrt(PROJ)).astype(jnp.bfloat16)


def setup_inputs(seed: int = 0) -> dict:
    key_list = jax.random.split(jax.random.key(seed), 4)
    first_view = draw_first_view(jax.random.fold_in(key_list[3], 71), 0)
    second_view = draw_second_view(jax.random.fold_in(key_list[3], 71), 0)
    projector = draw_projector(jax.random.fold_in(key_list[3], 71), 0)
    return {"first_view": first_view, "second_view": second_view, "projector": projector}


off_weight = 0.0051
epsilon = 1e-05

def standardize(values):
    average = lax.optimization_barrier(jnp.mean(values, axis=0, keepdims=True))
    centred = values - average
    spread = lax.optimization_barrier(jnp.mean(centred * centred, axis=0, keepdims=True))
    return centred * lax.rsqrt(spread + epsilon)

def reference(first_view, second_view, projector):
    first_std = standardize(jnp.dot(first_view, projector, preferred_element_type=jnp.float32))
    second_std = standardize(jnp.dot(second_view, projector, preferred_element_type=jnp.float32))
    clip_count = first_std.shape[0]
    blocks = 16
    stride = PROJ // blocks
    first_blocks = first_std.reshape(clip_count, blocks, stride).transpose(1, 0, 2)
    identity = jnp.eye(stride, dtype=jnp.float32)
    highest = lax.Precision.HIGHEST

    def step(carry, inputs):
        index, first_part = inputs
        correlation = jnp.dot(first_part.T, second_std, precision=highest, preferred_element_type=jnp.float32) / clip_count
        offset = (index * stride).astype(jnp.int32)
        zero = jnp.zeros((), jnp.int32)
        diag_block = lax.dynamic_slice(correlation, (zero, offset), (stride, stride))
        coupling = lax.dynamic_update_slice(2.0 * off_weight * correlation, 2.0 * off_weight * diag_block + identity * ((2.0 - 2.0 * off_weight) * diag_block - 2.0), (zero, offset))
        grad_part = jnp.dot(second_std, coupling.T, precision=highest, preferred_element_type=jnp.float32)
        carry = carry + jnp.dot(first_part, coupling, precision=highest, preferred_element_type=jnp.float32)
        return (carry, (grad_part, correlation))
    start_carry = jnp.zeros((clip_count, PROJ), jnp.float32)
    grad_two, (parts, corr_parts) = lax.scan(step, start_carry, (jnp.arange(blocks, dtype=jnp.int32), first_blocks))
    grad_one = parts.transpose(1, 0, 2).reshape(clip_count, PROJ)
    shard = PROJ // (N_ROW * N_COL)
    out_shape = (clip_count, N_COL, N_ROW, shard)
    corr_full = corr_parts.reshape(N_COL, N_ROW, shard, PROJ)
    return (grad_one.reshape(out_shape), grad_two.reshape(out_shape), corr_full)
```

```python
import functools

import jax
import jax.numpy as jnp
from jax import lax
from jax.experimental import pallas as pl
from jax.experimental.pallas import tpu as pltpu
from jax.sharding import PartitionSpec as P

off_weight = 0.0051
epsilon = 1e-05
VMEM_BYTES = 60 * 1024 * 1024


def other(index, bit):
    return index + bit - 2 * bit * lax.rem(lax.div(index, bit), 2)


def flipped(index, digits):
    bit = 1
    while bit <= digits:
        if digits & bit:
            index = other(index, bit)
        bit *= 2
    return index


def exchange_kernel(
    n_row, n_col,
    first_ref, second_ref, projector_ref,
    first_std, second_std, first_all, second_all,
    views, weights, partial, from_core, from_chip,
    load_sem, core_send, core_recv, chip_send, chip_recv,
    line_send, line_recv, gather_send, gather_recv, local_sem,
):
    me = lax.axis_index("row")
    here = lax.axis_index("col")
    clips, stride = first_std.shape
    half = clips // 2
    bits = [2**i for i in range(1, n_row.bit_length() - 1)]
    orders = (bits, bits[::-1])
    evens = sorted(range(0, n_row, 2), key=lambda d: (-bin(d).count("1"), d))
    stds = (first_std, second_std)

    view_loads = [
        pltpu.make_async_copy(ref, views.at[v], load_sem.at[n_row + v])
        for v, ref in enumerate((first_ref, second_ref))
    ]
    weight_loads = {}
    for e in evens:
        for d in (e + 1, e):
            column = pl.multiple_of(flipped(me, d) * stride, stride)
            weight_loads[d] = pltpu.make_async_copy(
                projector_ref.at[:, pl.ds(column, stride)], weights.at[d], load_sem.at[d]
            )
    view_loads[0].start()
    for load in weight_loads.values():
        load.start()
    view_loads[1].start()

    barrier = pltpu.get_barrier_semaphore()
    for bit in [1] + bits:
        pl.semaphore_signal(barrier, inc=1, device_id={"row": other(me, bit)})

    for move in {1, n_col - 1}:
        target = lax.rem(here + move, n_col)
        pl.semaphore_signal(barrier, inc=1, device_id={"col": target})
    pl.semaphore_wait(barrier, 1 + len(bits) + len({1, n_col - 1}))

    sent = []

    slots = {}
    for h in range(2):
        active = list(evens)
        for bit in orders[h]:
            active = [d for d in active if not d & bit]
            for d in active:
                slots[h, bit, d] = len([k for k in slots if k[0] == h])

    def rows(h):
        return pl.ds(h * half, half)

    def project(v, d):
        partial[v, d] = jnp.dot(views[v], weights[d], preferred_element_type=jnp.float32)

    def core_copy(v, e):
        return pltpu.make_async_remote_copy(
            src_ref=partial.at[v, e + 1],
            dst_ref=from_core.at[v, e // 2],
            send_sem=core_send.at[v, e // 2],
            recv_sem=core_recv.at[v, e // 2],
            device_id={"row": other(me, 1)},
        )

    def chip_copy(v, h, bit, d):
        slot = slots[h, bit, d ^ bit]
        return pltpu.make_async_remote_copy(
            src_ref=partial.at[v, d, rows(h)],
            dst_ref=from_chip.at[v, h, slot],
            send_sem=chip_send.at[v, h, slot],
            recv_sem=chip_recv.at[v, h, slot],
            device_id={"row": other(me, bit)},
        )

    def start(copy):
        copy.start()
        sent.append(copy)

    def add_core(v, e):
        core_copy(v, e).wait_recv()
        partial[v, e] += from_core[v, e // 2]

    def send_chip(v, h, step):
        bit = orders[h][step]
        done = sum(orders[h][:step])
        for d in evens:
            if d & bit and not d & done:
                start(chip_copy(v, h, bit, d))

    def add_chip(v, h, step, chosen):
        bit = orders[h][step]
        done = sum(orders[h][: step + 1])
        for d in evens:
            if not d & done and chosen(d):
                chip_copy(v, h, bit, d ^ bit).wait_recv()
                partial[v, d, rows(h)] += from_chip[v, h, slots[h, bit, d]]

    def project_all(v, send):
        def finish(e):
            add_core(v, e)
            if send:
                for h in range(2):
                    if e & orders[h][0]:
                        start(chip_copy(v, h, orders[h][0], e))

        before = None
        view_loads[v].wait()
        for e in evens:
            if v == 0:
                weight_loads[e + 1].wait()
            project(v, e + 1)
            start(core_copy(v, e))
            if before is not None:
                finish(before)
            if v == 0:
                weight_loads[e].wait()
            project(v, e)
            before = e
        finish(before)

    def reduce_rest(v, between=lambda: None):
        n = len(bits)
        for step in range(n - 1):
            for h in range(2):
                following = orders[h][step + 1]
                done = sum(orders[h][: step + 1])
                add_chip(v, h, step, lambda d: d & following)
                send_chip(v, h, step + 1)
            for h in range(2):
                following = orders[h][step + 1]
                add_chip(v, h, step, lambda d: not d & following)
        between()
        for h in range(2):
            add_chip(v, h, n - 1, lambda d: True)

    def standardize(v):
        values = partial[v, 0]
        centred = values - jnp.mean(values, axis=0, keepdims=True)
        spread = jnp.mean(centred * centred, axis=0, keepdims=True)
        stds[v][...] = centred * lax.rsqrt(spread + epsilon)

    def line_copy(way, step):
        block = here - step if way == 0 else here + step
        target = here + 1 if way == 0 else here - 1
        there = (here >= step) & (here < n_col - 1) if way == 0 else (
            (here + step < n_col) & (here > 0)
        )
        copy = pltpu.make_async_remote_copy(
            src_ref=first_std if step == 0 else first_all.at[block],
            dst_ref=first_all.at[block],
            send_sem=line_send.at[way, step],
            recv_sem=line_recv.at[way, step],
            device_id={"col": target},
        )
        return there, copy

    def line_arrives(way, step):
        return here - step - 1 >= 0 if way == 0 else here + step + 1 < n_col

    def line_step(step):
        for way in range(2):
            if step > 0:
                line_wait(way, step - 1)
            there, copy = line_copy(way, step)
            pl.when(there)(copy.start)

    def line_wait(way, step):
        block = here - step - 1 if way == 0 else here + step + 1

        @pl.when(line_arrives(way, step))
        def _():
            pltpu.make_async_remote_copy(
                src_ref=first_std,
                dst_ref=first_all.at[block],
                send_sem=line_send.at[way, step],
                recv_sem=line_recv.at[way, step],
                device_id={"col": here - 1 if way == 0 else here + 1},
            ).wait_recv()

    def gather_copy(h, bit, d):
        block = flipped(me, d)
        src = second_std.at[rows(h)] if d == 0 else second_all.at[block, rows(h)]
        return pltpu.make_async_remote_copy(
            src_ref=src,
            dst_ref=second_all.at[block, rows(h)],
            send_sem=gather_send.at[h, d + bit - 1],
            recv_sem=gather_recv.at[h, d + bit - 1],
            device_id={"row": other(me, bit)},
        )

    def gather_wait(h, e, bit):
        pltpu.make_async_remote_copy(
            src_ref=second_std.at[rows(h)],
            dst_ref=second_all.at[flipped(me, e), rows(h)],
            send_sem=gather_send.at[h, e - 1],
            recv_sem=gather_recv.at[h, e - 1],
            device_id={"row": other(me, bit)},
        ).wait_recv()

    def gather_available(h, d, step):
        for bit in orders[h][step:] + [1]:
            start(gather_copy(h, bit, d))

    project_all(0, True)
    project_all(1, False)

    def begin_second():
        for e in evens:
            for h in range(2):
                if e & orders[h][0]:
                    start(chip_copy(1, h, orders[h][0], e))

    reduce_rest(0, begin_second)
    standardize(0)
    own_first = pltpu.make_async_copy(first_std, first_all.at[here], local_sem.at[0])
    own_first.start()
    line_step(0)
    middle = [lambda s=s: line_step(s) for s in range(1, n_col - 1)]
    reduce_rest(1, middle[0] if middle else lambda: None)
    standardize(1)
    own_second = pltpu.make_async_copy(second_std, second_all.at[me], local_sem.at[1])
    own_second.start()
    for h in range(2):
        gather_available(h, 0, 0)
    waiting = list(middle[1:])
    for step in range(len(bits)):
        for h in range(2):
            bit = orders[h][step]
            have = [d for d in range(0, n_row, 2) if not d & ~sum(orders[h][:step])]
            for d in have:
                gather_wait(h, d + bit, bit)
                gather_available(h, d + bit, step + 1)
        if waiting:
            waiting.pop(0)()
    for action in waiting:
        action()
    for h in range(2):
        for d in range(0, n_row, 2):
            gather_wait(h, d + 1, 1)
    for way in range(2):
        line_wait(way, n_col - 2)
    for copy in sent:
        copy.wait_send()
    for way in range(2):
        for step in range(n_col - 1):
            there, copy = line_copy(way, step)
            pl.when(there)(copy.wait_send)
    own_first.wait()
    own_second.wait()


def exchange(first_view, second_view, projector, n_row, n_col):
    clips, depth = first_view.shape
    stride = projector.shape[1] // n_row
    full = jax.ShapeDtypeStruct((clips, stride), jnp.float32)
    anywhere = pl.BlockSpec(memory_space=pl.ANY)
    inside = pl.BlockSpec(memory_space=pltpu.VMEM)
    dma = pltpu.SemaphoreType.DMA
    pairs = n_row // 2
    return pl.pallas_call(
        functools.partial(exchange_kernel, n_row, n_col),
        out_shape=(
            full,
            full,
            jax.ShapeDtypeStruct((n_col, clips, stride), jnp.float32),
            jax.ShapeDtypeStruct((n_row, clips, stride), jnp.float32),
        ),
        in_specs=[anywhere] * 3,
        out_specs=(inside, inside, anywhere, anywhere),
        scratch_shapes=[
            pltpu.VMEM((2, clips, depth), jnp.bfloat16),
            pltpu.VMEM((n_row, depth, stride), jnp.bfloat16),
            pltpu.VMEM((2, n_row, clips, stride), jnp.float32),
            pltpu.VMEM((2, pairs, clips, stride), jnp.float32),
            pltpu.VMEM((2, 2, pairs - 1, clips // 2, stride), jnp.float32),
            dma((n_row + 2,)),
            dma((2, pairs)),
            dma((2, pairs)),
            dma((2, 2, pairs - 1)),
            dma((2, 2, pairs - 1)),
            dma((2, n_col - 1)),
            dma((2, n_col - 1)),
            dma((2, n_row - 1)),
            dma((2, n_row - 1)),
            dma((2,)),
        ],
        compiler_params=pltpu.CompilerParams(
            collective_id=0, has_side_effects=True, vmem_limit_bytes=VMEM_BYTES
        ),
        cost_estimate=pl.CostEstimate(
            flops=4 * clips * depth * projector.shape[1],
            bytes_accessed=2 * projector.size,
            transcendentals=0,
        ),
        name="exchange",
    )(first_view, second_view, projector)


def split(values):
    high = values.astype(jnp.bfloat16)
    return high, (values - high.astype(jnp.float32)).astype(jnp.bfloat16)


def correlate_kernel(first_ref, second_ref, out_ref, first_high, first_low):
    n_col, clips, stride = first_ref.shape

    @pl.when(pl.program_id(0) == 0)
    def _():
        for c in range(n_col):
            high, low = split(first_ref[c].T)
            first_high[c] = high
            first_low[c] = low

    high, low = split(second_ref[0])
    for c in range(n_col):
        total = jnp.dot(first_high[c], high, preferred_element_type=jnp.float32)
        total += jnp.dot(first_high[c], low, preferred_element_type=jnp.float32)
        total += jnp.dot(first_low[c], high, preferred_element_type=jnp.float32)
        out_ref[c, 0] = total / clips


def correlate(first_all, second_all):
    n_col, clips, stride = first_all.shape
    n_row = second_all.shape[0]
    return pl.pallas_call(
        correlate_kernel,
        grid=(n_row,),
        out_shape=jax.ShapeDtypeStruct((n_col, 1, stride, n_row * stride), jnp.float32),
        in_specs=[
            pl.BlockSpec((n_col, clips, stride), lambda r: (0, 0, 0)),
            pl.BlockSpec((1, clips, stride), lambda r: (r, 0, 0)),
        ],
        out_specs=pl.BlockSpec((n_col, 1, stride, stride), lambda r: (0, 0, 0, r)),
        scratch_shapes=[pltpu.VMEM((n_col, stride, clips), jnp.bfloat16)] * 2,
        compiler_params=pltpu.CompilerParams(vmem_limit_bytes=40 * 1024 * 1024),
        cost_estimate=pl.CostEstimate(
            flops=6 * clips * n_col * n_row * stride * stride,
            bytes_accessed=4 * n_col * n_row * stride * stride,
            transcendentals=0,
        ),
        name="correlate",
    )(first_all, second_all)


def shards(first_view, second_view, projector):
    n_row, n_col = lax.axis_size("row"), lax.axis_size("col")
    clips = first_view.shape[0]
    first_std, second_std, first_all, second_all = exchange(
        first_view, second_view, projector, n_row, n_col
    )
    stride = first_std.shape[1]
    high = lax.Precision.HIGH

    def gram(values):
        return lax.dot_general(
            values, values, (((1,), (1,)), ((), ())),
            precision=high, preferred_element_type=jnp.float32,
        )

    first_gram, second_gram = lax.psum((gram(first_std), gram(second_std)), ("row", "col"))
    corr_out = correlate(first_all, second_all)
    diag_corr = jnp.sum(first_std * second_std, axis=0, keepdims=True) / clips
    diag_term = (2.0 - 2.0 * off_weight) * diag_corr - 2.0
    factor = 2.0 * off_weight / clips

    def product(matrix, values):
        return factor * jnp.dot(
            matrix, values, precision=high, preferred_element_type=jnp.float32
        )

    grad_one = product(second_gram, first_std) + second_std * diag_term
    grad_two = product(first_gram, second_std) + first_std * diag_term
    return (
        grad_one.reshape(clips, 1, 1, stride),
        grad_two.reshape(clips, 1, 1, stride),
        corr_out,
    )


def solution(mesh):
    in_specs = (P(None, "row"), P(None, "row"), P("row", "col"))
    out_specs = (
        P(None, "col", "row", None),
        P(None, "col", "row", None),
        P(None, "row", None, "col"),
    )
    return jax.shard_map(shards, mesh=mesh, in_specs=in_specs, out_specs=out_specs, check_vma=False)
```
